256 devices in a mesh: row: 32 (over y, z), col: 8 (over x, core).
Axes of the slice: x: 4, y: 4, z: 8, core: 2. Of those that a mesh axis runs over, the one named last changes fastest.
Arguments:
- factor: float32 [1, 32, 4, 8, 128, 128], P(None, 'row', None, 'col'), may hold values from -0.046875 to 0.046875
- pattern: int32 [1, 32, 4, 8], P(None, 'row', None, 'col'), may hold values 0 or 1
- inverse: float32 [32, 128, 128], replicated, may hold values from -2 to 2
- rhs: float32 [1, 32, 128, 128], P(None, 'row'), may hold values from -6 to 6
Outputs:
- forward_out: float32 [1, 32, 128, 128], P(None, 'row')
- backward_out: float32 [1, 32, 128, 128], P(None, 'row')
The draws below stay inside these ranges and needn't reach their ends.
All inputs are finite; a program needn't handle non-finite values. No bound on the sum of `pattern` on one device may be relied on, other than what follows from the above.
Results may differ from the reference program's by a relative error of at most 0.0001.
Values sent between devices are 32-bit elements; how exact they have to be, the bound alone decides.
A program may use at most 64 MiB of HBM per device.

```python
import jax
import jax.numpy as jnp
from jax import lax

PANEL = 128
NRHS = 128
BLK_ROW = 1
BLOCKS = 32
BLK_COL = 4
N_ROW = 32
N_COL = 8


def draw_inverse(key, part):
    key = jax.random.fold_in(key, 5)
    first, second = jax.random.split(key)
    diagonal = jax.random.uniform(first, (BLOCKS, PANEL), jnp.float32, 0.5, 1.5)
    spread = jax.random.truncated_normal(second, -6.0, 6.0, (BLOCKS, PANEL, PANEL), jnp.float32) * (0.6 / PANEL ** 0.5)
    return spread + diagonal[:, :, None] * jnp.eye(PANEL, dtype=jnp.float32)[None]


def plant(drawn, key, smallest, top_value):
    index_at = [jax.random.randint(jax.random.fold_in(key, axis), (), 0, length) for axis, length in enumerate(drawn.shape)]
    longest = drawn.shape.index(max(drawn.shape))
    neighbour = index_at[:longest] + [(index_at[longest] + 1) % drawn.shape[longest]] + index_at[longest + 1:]
    return drawn.at[tuple(index_at)].set(smallest).at[tuple(neighbour)].set(top_value)


def block_levels(key, shape, shards, low, high):
    gain, own = 1.0, jax.random.fold_in(key, 6)
    for position, shards_of in shards:
        heights = jnp.exp(jax.random.uniform(jax.random.fold_in(own, position), (shards_of,), jnp.float32, low / len(shards), high / len(shards)))
        gain = gain * jnp.repeat(heights, shape[position] // shards_of).reshape([-1 if axis == position else 1 for axis in range(len(shape))])
    return gain


def centred(stream_key, extent, scale, bound, pieces=(), held_as=jnp.bfloat16):
    values = jax.random.normal(stream_key, extent, jnp.float32) * scale
    if len(pieces) > 0:
        values = block_levels(stream_key, extent, pieces, -0.22, 0.18) * values
    return jnp.clip(values, min=-bound, max=bound).astype(held_as)


def setup_inputs(seed: int = 0) -> dict:
    seeds = jax.random.split(jax.random.key(seed), 5)
    return {
        "factor": centred(seeds[0], (BLK_ROW, N_ROW, BLK_COL, N_COL, PANEL, PANEL), (4 * BLOCKS * PANEL) ** -0.5, 0.046875, ((1, 32), (3, 8)), jnp.float32),
        "pattern": plant((jax.random.randint(seeds[1], (BLK_ROW, N_ROW, BLK_COL, N_COL), 0, 4) < 3).astype(jnp.int32), jax.random.fold_in(seeds[1], 1), 0, 1),
        "inverse": draw_inverse(jax.random.fold_in(seeds[4], 71), 0),
        "rhs": centred(seeds[3], (BLK_ROW, N_ROW, PANEL, NRHS), 1.0, 6.0, ((1, 32),), jnp.float32),
    }


def reference(factor, pattern, inverse, rhs):
    blocks_total = BLK_ROW * N_ROW
    topmost_level = lax.Precision.HIGHEST
    panel_blocks = factor.reshape(blocks_total, blocks_total, PANEL, PANEL)
    order = jnp.arange(blocks_total) // N_COL
    lower = (order[:, None] > order[None, :]).astype(jnp.float32)
    active_blocks = pattern.reshape(blocks_total, blocks_total).astype(jnp.float32) * lower
    right = rhs.reshape(blocks_total, PANEL, NRHS)

    def forward(destination_row, solved):
        update_term = jnp.einsum('k,kab,kbr->ar', active_blocks[destination_row], panel_blocks[destination_row], solved, precision=topmost_level)
        fresh = jnp.dot(inverse[destination_row], right[destination_row] - update_term, precision=topmost_level)
        return solved.at[destination_row].set(fresh)

    solved = lax.fori_loop(0, blocks_total, forward, jnp.zeros((blocks_total, PANEL, NRHS), jnp.float32))

    def backward(count, finished_blocks):
        destination_row = blocks_total - 1 - count
        update_term = jnp.einsum('f,fcy,fch->yh', active_blocks[:, destination_row], panel_blocks[:, destination_row], finished_blocks, precision=topmost_level)
        fresh = jnp.einsum('ab,ar->br', inverse[destination_row], solved[destination_row] - update_term, precision=topmost_level)
        return finished_blocks.at[destination_row].set(fresh)

    finished_blocks = lax.fori_loop(0, blocks_total, backward, jnp.zeros((blocks_total, PANEL, NRHS), jnp.float32))
    shape = (BLK_ROW, N_ROW, PANEL, NRHS)
    return solved.reshape(shape), finished_blocks.reshape(shape)
```

```python
import jax
import jax.numpy as jnp
from jax import lax
from jax.experimental import pallas as pl
from jax.experimental.pallas import tpu as pltpu
from jax.sharding import PartitionSpec as P

MESH = pl.DeviceIdType.MESH
F32 = jnp.float32
BF16 = jnp.bfloat16
LEVELS = 4
PER = 8
W = 128
S = W // PER
FAR_FIRST = (4, 3, 5, 2, 6, 1, 7, 0)


def halves(v):
    hi = v.astype(BF16)
    lo = (v - hi.astype(F32)).astype(BF16)
    return hi, lo


def quadrants(p, m, n):
    return p[:m, :n] + (p[m:, :n] + p[:m, n:])


def dot_nt(a, b):
    return lax.dot_general(a, b, (((1,), (1,)), ((), ())), preferred_element_type=F32)


def dot_nn(a, b):
    return lax.dot_general(a, b, (((1,), (0,)), ((), ())), preferred_element_type=F32)


def kernel(
    factor, pattern, inverse, rhs, y_out, x_out,
    d_in, l_in, b_in, b_t, m_in, m_hl, d_hl, dt_hl, y_in, p_in, y_own, u_own, t_own, y_all, u_all,
    load_sem, m_send, m_recv, m_relay, y_send, y_recv, p_send, p_recv, g_send, g_recv,
):
    row = lax.axis_index("row")
    col = lax.axis_index("col")
    level = row // PER
    z = row % PER
    x = col // 2
    h = col % 2

    def peer(dx, dh):
        return lax.rem(x + dx, 4) * 2 + lax.rem(h + dh, 2)

    col_peers = [peer(dx, dh) for dx, dh in ((2, 1), (2, 0), (1, 1), (3, 1), (1, 0), (3, 0), (0, 1))]

    load_d = pltpu.make_async_copy(inverse.at[row], d_in, load_sem.at[0])
    load_b = pltpu.make_async_copy(rhs.at[0, 0], b_in, load_sem.at[1])
    load_l = [pltpu.make_async_copy(factor.at[0, 0, k, 0], l_in.at[k], load_sem.at[2 + k]) for k in range(LEVELS - 1)]
    load_d.start()
    for k in range(LEVELS - 1):
        load_l[k].start()
    load_b.start()

    barrier = pltpu.get_barrier_semaphore()
    for dz in FAR_FIRST:
        for dy in (2, 1, 3):
            to = lax.rem(level + dy, LEVELS) * PER + lax.rem(z + dz, PER)
            pl.semaphore_signal(barrier, inc=1, device_id=(to, col), device_id_type=MESH)
    for c in col_peers:
        pl.semaphore_signal(barrier, inc=1, device_id=(row, c), device_id_type=MESH)

    load_d.wait()
    d = d_in[...]
    dh_, dl_ = halves(d)
    d_hl[:W, :] = dh_
    d_hl[W:, :] = dl_
    th, tl = halves(jnp.transpose(d))
    dt_hl[:W, :] = th
    dt_hl[W:, :] = tl
    for k in range(LEVELS - 1):
        load_l[k].wait()
        keep = jnp.where(level > k, pattern[0, k].astype(F32), 0.0)
        lh, ll = halves(l_in[k] * keep)
        m_in[k, col] = quadrants(dot_nn(d_hl[...], jnp.concatenate([lh, ll], axis=1)), W, W)
    load_b.wait()
    b_t[...] = jnp.transpose(b_in[...])
    bh, bl = halves(b_t[pl.ds(pl.multiple_of(col * S, S), S), :])
    start = quadrants(dot_nt(jnp.concatenate([bh, bl], axis=0), d_hl[...]), S, W)
    y_own[...] = start
    pl.semaphore_wait(barrier, 31)

    def wait(ref, sem):
        pltpu.make_async_copy(ref, ref, sem).wait()

    def send(src, dst, ssem, rsem, to_row, to_col):
        pltpu.make_async_remote_copy(
            src_ref=src, dst_ref=dst, send_sem=ssem, recv_sem=rsem, device_id=(to_row, to_col), device_id_type=MESH
        ).start()

    def to_level(src_of, dst, ssem, rsem, target):
        for dz in FAR_FIRST:
            zt = lax.rem(z + dz, PER)
            send(src_of(zt), dst, ssem, rsem, target * PER + zt, col)

    def to_col(own, dst, which):
        for c in col_peers:
            send(own, dst, g_send.at[which], g_recv.at[which], row, c)

    for lev in range(LEVELS):

        @pl.when(level == lev)
        def _(lev=lev):
            if lev == 0:
                for target in range(1, LEVELS):
                    to_level(lambda zt: y_own, y_in.at[0, z], y_send, y_recv.at[0], target)
            for k in range(lev):
                own = m_in.at[k, col]
                for i, dx in enumerate((2, 1, 3)):
                    send(own, own, m_send, m_recv.at[k, i], row, peer(dx, 0))
                send(own, own, m_send, m_relay.at[k], row, peer(0, 1))
            for k in range(lev):
                for i, dx in ((1, 1), (2, 3), (0, 2)):
                    got = m_in.at[k, peer(4 - dx, 0)]
                    wait(got, m_recv.at[k, i])
                    send(got, got, m_send, m_relay.at[k], row, peer(0, 1))
                wait(m_in.at[k, pl.ds(0, 4)], m_relay.at[k])
                for c in range(PER):
                    mh, ml = halves(m_in[k, c])
                    m_hl[k, :W, c * W:(c + 1) * W] = mh
                    m_hl[k, W:, c * W:(c + 1) * W] = ml
            acc = start
            for k in range(lev):
                wait(y_in.at[k], y_recv.at[k])
                parts = [halves(y_in[k, c]) for c in range(PER)]
                lhs = jnp.concatenate(
                    [jnp.concatenate([p[0] for p in parts], axis=1), jnp.concatenate([p[1] for p in parts], axis=1)], axis=0
                )
                acc = acc - quadrants(dot_nt(lhs, m_hl[k]), S, W)
            if lev > 0:
                y_own[...] = acc
                for target in range(lev + 1, LEVELS):
                    to_level(lambda zt: y_own, y_in.at[lev, z], y_send, y_recv.at[lev], target)
            if lev < LEVELS - 1:
                y_all[col] = acc
                to_col(y_own, y_all.at[col], 0)
            for up in range(LEVELS - 1, lev, -1):
                wait(p_in.at[up - 1], p_recv.at[up - 1])
                total = p_in[up - 1, 0]
                for c in range(1, PER):
                    total = total + p_in[up - 1, c]
                acc = acc - total
            u_own[...] = acc
            uh, ul = halves(acc)
            lhs = jnp.concatenate(
                [jnp.concatenate([uh, uh], axis=1), jnp.concatenate([ul, jnp.zeros_like(ul)], axis=1)], axis=0
            )
            for k in range(lev - 1, -1, -1):
                t = dot_nn(lhs, m_hl[k])
                t = t[:S] + t[S:]
                for c in range(PER):
                    t_own[k, c] = t[:, c * W:(c + 1) * W]
                to_level(lambda zt: t_own.at[k, zt], p_in.at[lev - 1, z], p_send, p_recv.at[lev - 1], k)
            if lev == LEVELS - 1:
                y_all[col] = acc
                to_col(y_own, y_all.at[col], 0)
            u_all[col] = acc
            to_col(u_own, u_all.at[col], 1)

            wait(y_all.at[pl.ds(0, PER - 1)], g_recv.at[0])
            y_out[0, 0] = jnp.transpose(y_all[...].reshape(W, W))
            wait(u_all.at[pl.ds(0, PER - 1)], g_recv.at[1])
            ah, al = halves(u_all[...].reshape(W, W))
            x_out[0, 0] = quadrants(dot_nt(dt_hl[...], jnp.concatenate([ah, al], axis=0)), W, W)

            for k in range(lev):
                wait(m_in.at[k, pl.ds(0, 7)], m_send)
                wait(t_own.at[k], p_send)
            for _ in range(lev + 1, LEVELS):
                wait(y_in.at[0], y_send)
            for which in range(2):
                wait(y_all.at[pl.ds(0, PER - 1)], g_send.at[which])


def shards(factor, pattern, inverse, rhs):
    out = jax.ShapeDtypeStruct((1, 1, W, W), F32)
    dma = pltpu.SemaphoreType.DMA
    return pl.pallas_call(
        kernel,
        out_shape=(out, out),
        in_specs=[
            pl.BlockSpec(memory_space=pltpu.HBM),
            pl.BlockSpec(memory_space=pltpu.SMEM),
            pl.BlockSpec(memory_space=pltpu.HBM),
            pl.BlockSpec(memory_space=pltpu.HBM),
        ],
        out_specs=(pl.BlockSpec(memory_space=pltpu.VMEM), pl.BlockSpec(memory_space=pltpu.VMEM)),
        scratch_shapes=[
            pltpu.VMEM((W, W), F32),
            pltpu.VMEM((LEVELS - 1, W, W), F32),
            pltpu.VMEM((W, W), F32),
            pltpu.VMEM((W, W), F32),
            pltpu.VMEM((LEVELS - 1, PER, W, W), F32),
            pltpu.VMEM((LEVELS - 1, 2 * W, PER * W), BF16),
            pltpu.VMEM((2 * W, W), BF16),
            pltpu.VMEM((2 * W, W), BF16),
            pltpu.VMEM((LEVELS - 1, PER, S, W), F32),
            pltpu.VMEM((LEVELS - 1, PER, S, W), F32),
            pltpu.VMEM((S, W), F32),
            pltpu.VMEM((S, W), F32),
            pltpu.VMEM((LEVELS - 1, PER, S, W), F32),
            pltpu.VMEM((PER, S, W), F32),
            pltpu.VMEM((PER, S, W), F32),
            dma((LEVELS + 1,)),
            dma,
            dma((LEVELS - 1, 3)),
            dma((LEVELS - 1,)),
            dma,
            dma((LEVELS - 1,)),
            dma,
            dma((LEVELS - 1,)),
            dma((2,)),
            dma((2,)),
        ],
        compiler_params=pltpu.CompilerParams(collective_id=0, has_side_effects=True, vmem_limit_bytes=60 * 2**20),
        name="solve",
    )(factor, pattern.reshape(1, LEVELS), inverse, rhs)


def solution(mesh):
    return jax.shard_map(
        shards,
        mesh=mesh,
        in_specs=(
            P(None, "row", None, "col", None, None),
            P(None, "row", None, "col"),
            P(),
            P(None, "row", None, None),
        ),
        out_specs=(P(None, "row", None, None), P(None, "row", None, None)),
        check_vma=False,
    )
```

```python
import jax
import jax.numpy as jnp
from jax import lax
from jax.experimental import pallas as pl
from jax.experimental.pallas import tpu as pltpu
from jax.sharding import PartitionSpec as P

MESH = pl.DeviceIdType.MESH
F32 = jnp.float32
BF16 = jnp.bfloat16
LEVELS = 4
PER = 8
W = 128
SLICES = 4
S = W // SLICES
FAR_FIRST = (4, 3, 5, 2, 6, 1, 7, 0)


def halves(v):
    hi = v.astype(BF16)
    lo = (v - hi.astype(F32)).astype(BF16)
    return hi, lo


def quadrants(p, m, n):
    return p[:m, :n] + (p[m:, :n] + p[:m, n:])


def dot_nt(a, b):
    return lax.dot_general(a, b, (((1,), (1,)), ((), ())), preferred_element_type=F32)


def dot_nn(a, b):
    return lax.dot_general(a, b, (((1,), (0,)), ((), ())), preferred_element_type=F32)


def kernel(
    factor, pattern, inverse, rhs, y_out, x_out,
    d_in, l_in, b_in, b_t, m_in, m_hl, d_hl, dt_hl, y_in, p_in, y_own, u_own, t_own, y_all, u_all,
    load_sem, m_send, m_recv, y_send, y_recv, p_send, p_recv, g_send, g_recv,
):
    row = lax.axis_index("row")
    col = lax.axis_index("col")
    level = row // PER
    z = row % PER
    x = col // 2
    solver = col % 2 == 1

    load_d = pltpu.make_async_copy(inverse.at[row], d_in, load_sem.at[0])
    load_b = pltpu.make_async_copy(rhs.at[0, 0], b_in, load_sem.at[1])
    load_l = [pltpu.make_async_copy(factor.at[0, 0, k, 0], l_in.at[k], load_sem.at[2 + k]) for k in range(LEVELS - 1)]
    load_d.start()
    load_l[0].start()

    def peer(dx, h):
        return lax.rem(x + dx, SLICES) * 2 + h

    barrier = pltpu.get_barrier_semaphore()

    def signal(to_row, to_col):
        pl.semaphore_signal(barrier, inc=1, device_id=(to_row, to_col), device_id_type=MESH)

    @pl.when(solver & (level > 0))
    def _():
        for dz in FAR_FIRST:
            signal(lax.rem(z + dz, PER), col)

    @pl.when(solver)
    def _():
        for dx in (2, 1, 3):
            signal(row, peer(dx, 1))
        for dx in (2, 1, 3, 0):
            signal(row, peer(dx, 0))

    @pl.when(jnp.logical_not(solver))
    def _():
        for dx in (2, 1, 3, 0):
            signal(row, peer(dx, 1))

    load_b.start()
    for k in range(1, LEVELS - 1):
        load_l[k].start()

    def wait(ref, sem):
        pltpu.make_async_copy(ref, ref, sem).wait()

    def send(src, dst, ssem, rsem, to_row, to_col):
        pltpu.make_async_remote_copy(
            src_ref=src, dst_ref=dst, send_sem=ssem, recv_sem=rsem, device_id=(to_row, to_col), device_id_type=MESH
        ).start()

    def to_level(src_of, dst, ssem, rsem, target):
        for dz in FAR_FIRST:
            zt = lax.rem(z + dz, PER)
            send(src_of(zt), dst, ssem, rsem, target * PER + zt, col)

    def to_row(own, all_, which):
        all_[x] = own[...]
        for dx, h in ((2, 0), (2, 1), (1, 0), (3, 0), (1, 1), (3, 1), (0, 0)):
            send(own, all_.at[x], g_send.at[which], g_recv.at[which], row, peer(dx, h))

    load_d.wait()
    dh_, dl_ = halves(d_in[...])
    d_hl[:W, :] = dh_
    d_hl[W:, :] = dl_

    def form(k):
        load_l[k].wait()
        lh, ll = halves(l_in[k] * pattern[0, k].astype(F32))
        m_in[k, col] = quadrants(dot_nn(d_hl[...], jnp.concatenate([lh, ll], axis=1)), W, W)

    def turn():
        th, tl = halves(jnp.transpose(d_in[...]))
        dt_hl[:W, :] = th
        dt_hl[W:, :] = tl

    def finish(messages):
        wait(y_all.at[pl.ds(0, messages)], g_recv.at[0])
        y_out[0, 0] = jnp.transpose(y_all[...].reshape(W, W))
        wait(u_all.at[pl.ds(0, messages)], g_recv.at[1])
        ah, al = halves(u_all[...].reshape(W, W))
        x_out[0, 0] = quadrants(dot_nt(dt_hl[...], jnp.concatenate([ah, al], axis=0)), W, W)

    @pl.when(jnp.logical_not(solver))
    def _():
        for k in range(LEVELS - 1):

            @pl.when(level > k)
            def _(k=k):
                form(k)
                if k == 0:
                    pl.semaphore_wait(barrier, SLICES)
                own = m_in.at[k, col]
                for dx in (2, 1, 3, 0):
                    send(own, own, m_send, m_recv.at[k], row, peer(dx, 1))

            @pl.when(level <= k)
            def _(k=k):
                load_l[k].wait()

        @pl.when(level == 0)
        def _():
            pl.semaphore_wait(barrier, SLICES)

        load_b.wait()
        turn()
        finish(SLICES)
        for k in range(LEVELS - 1):

            @pl.when(level > k)
            def _(k=k):
                wait(m_in.at[k, pl.ds(0, SLICES)], m_send)

    def first_term():
        load_b.wait()
        b_t[...] = jnp.transpose(b_in[...])
        bh, bl = halves(b_t[pl.ds(pl.multiple_of(x * S, S), S), :])
        return quadrants(dot_nt(jnp.concatenate([bh, bl], axis=0), d_hl[...]), S, W)

    for lev in range(LEVELS):

        @pl.when(solver & (level == lev))
        def _(lev=lev):
            if lev == 0:
                start = first_term()
                y_own[...] = start
                pl.semaphore_wait(barrier, 31)
                for target in range(1, LEVELS):
                    to_level(lambda zt: y_own, y_in.at[0, z], y_send, y_recv.at[0], target)
            for k in range(lev, LEVELS - 1):
                load_l[k].wait()
            for k in range(lev):
                form(k)
                if k == 0:
                    pl.semaphore_wait(barrier, 7)
                own = m_in.at[k, col]
                for dx in (2, 1, 3):
                    send(own, own, m_send, m_recv.at[k], row, peer(dx, 1))
            if lev > 0:
                start = first_term()
            turn()
            for k in range(lev):
                wait(m_in.at[k, pl.ds(0, PER - 1)], m_recv.at[k])
                for c in range(PER):
                    mh, ml = halves(m_in[k, c])
                    m_hl[k, :W, c * W:(c + 1) * W] = mh
                    m_hl[k, W:, c * W:(c + 1) * W] = ml
            acc = start
            for k in range(lev):
                wait(y_in.at[k], y_recv.at[k])
                parts = [halves(y_in[k, c]) for c in range(PER)]
                lhs = jnp.concatenate(
                    [jnp.concatenate([p[0] for p in parts], axis=1), jnp.concatenate([p[1] for p in parts], axis=1)], axis=0
                )
                acc = acc - quadrants(dot_nt(lhs, m_hl[k]), S, W)
            if lev > 0:
                y_own[...] = acc
                for target in range(lev + 1, LEVELS):
                    to_level(lambda zt: y_own, y_in.at[lev, z], y_send, y_recv.at[lev], target)
            if lev < LEVELS - 1:
                to_row(y_own, y_all, 0)
            for up in range(LEVELS - 1, lev, -1):
                wait(p_in.at[up - 1], p_recv.at[up - 1])
                total = p_in[up - 1, 0]
                for c in range(1, PER):
                    total = total + p_in[up - 1, c]
                acc = acc - total
            u_own[...] = acc
            uh, ul = halves(acc)
            lhs = jnp.concatenate(
                [jnp.concatenate([uh, uh], axis=1), jnp.concatenate([ul, jnp.zeros_like(ul)], axis=1)], axis=0
            )
            for k in range(lev - 1, -1, -1):
                t = dot_nn(lhs, m_hl[k])
                t = t[:S] + t[S:]
                for c in range(PER):
                    t_own[k, c] = t[:, c * W:(c + 1) * W]
                to_level(lambda zt: t_own.at[k, zt], p_in.at[lev - 1, z], p_send, p_recv.at[lev - 1], k)
            if lev == LEVELS - 1:
                to_row(y_own, y_all, 0)
            to_row(u_own, u_all, 1)
            finish(SLICES - 1)

            for k in range(lev):
                wait(m_in.at[k, pl.ds(0, SLICES - 1)], m_send)
                wait(t_own.at[k], p_send)
            for _ in range(lev + 1, LEVELS):
                wait(y_in.at[0], y_send)
            for which in range(2):
                wait(y_in.at[0, pl.ds(0, 7)], g_send.at[which])


def put(y, x, y_out, x_out, sem):
    a = pltpu.make_async_copy(y, y_out, sem.at[0])
    b = pltpu.make_async_copy(x, x_out, sem.at[1])
    a.start()
    b.start()
    a.wait()
    b.wait()


def shards(factor, pattern, inverse, rhs):
    out = jax.ShapeDtypeStruct((1, 1, W, W), F32)
    dma = pltpu.SemaphoreType.DMA
    y, x = pl.pallas_call(
        kernel,
        out_shape=(out, out),
        in_specs=[
            pl.BlockSpec(memory_space=pltpu.HBM),
            pl.BlockSpec(memory_space=pltpu.SMEM),
            pl.BlockSpec(memory_space=pltpu.HBM),
            pl.BlockSpec(memory_space=pltpu.HBM),
        ],
        out_specs=(pl.BlockSpec(memory_space=pltpu.VMEM), pl.BlockSpec(memory_space=pltpu.VMEM)),
        scratch_shapes=[
            pltpu.VMEM((W, W), F32),
            pltpu.VMEM((LEVELS - 1, W, W), F32),
            pltpu.VMEM((W, W), F32),
            pltpu.VMEM((W, W), F32),
            pltpu.VMEM((LEVELS - 1, PER, W, W), F32),
            pltpu.VMEM((LEVELS - 1, 2 * W, PER * W), BF16),
            pltpu.VMEM((2 * W, W), BF16),
            pltpu.VMEM((2 * W, W), BF16),
            pltpu.VMEM((LEVELS - 1, PER, S, W), F32),
            pltpu.VMEM((LEVELS - 1, PER, S, W), F32),
            pltpu.VMEM((S, W), F32),
            pltpu.VMEM((S, W), F32),
            pltpu.VMEM((LEVELS - 1, PER, S, W), F32),
            pltpu.VMEM((SLICES, S, W), F32),
            pltpu.VMEM((SLICES, S, W), F32),
            dma((LEVELS + 1,)),
            dma,
            dma((LEVELS - 1,)),
            dma,
            dma((LEVELS - 1,)),
            dma,
            dma((LEVELS - 1,)),
            dma((2,)),
            dma((2,)),
        ],
        compiler_params=pltpu.CompilerParams(collective_id=0, has_side_effects=True, vmem_limit_bytes=60 * 2**20),
        name="solve",
    )(factor, pattern.reshape(1, LEVELS), inverse, rhs)
    return pl.pallas_call(
        put,
        out_shape=(out, out),
        in_specs=[pl.BlockSpec(memory_space=pltpu.VMEM)] * 2,
        out_specs=(pl.BlockSpec(memory_space=pltpu.HBM),) * 2,
        scratch_shapes=[dma((2,))],
        name="put",
    )(y, x)


def solution(mesh):
    return jax.shard_map(
        shards,
        mesh=mesh,
        in_specs=(
            P(None, "row", None, "col", None, None),
            P(None, "row", None, "col"),
            P(),
            P(None, "row", None, None),
        ),
        out_specs=(P(None, "row", None, None), P(None, "row", None, None)),
        check_vma=False,
    )
```

```python
import jax
import jax.numpy as jnp
from jax import lax
from jax.experimental import pallas as pl
from jax.experimental.pallas import tpu as pltpu
from jax.sharding import PartitionSpec as P

MESH = pl.DeviceIdType.MESH
F32 = jnp.float32
BF16 = jnp.bfloat16
LEVELS = 4
PER = 8
W = 128
SLICES = 4
S = W // SLICES
FAR_FIRST = (4, 3, 5, 2, 6, 1, 7, 0)


def halves(v):
    hi = v.astype(BF16)
    lo = (v - hi.astype(F32)).astype(BF16)
    return hi, lo


def quadrants(p, m, n):
    return p[:m, :n] + (p[m:, :n] + p[:m, n:])


def dot_nt(a, b):
    return lax.dot_general(a, b, (((1,), (1,)), ((), ())), preferred_element_type=F32)


def dot_nn(a, b):
    return lax.dot_general(a, b, (((1,), (0,)), ((), ())), preferred_element_type=F32)


def kernel(
    factor, pattern, inverse, rhs, y_out, x_out,
    d_in, l_in, b_in, b_t, m_in, m_fwd, m_bwd, d_hl, dt_hl, y_in, p_in, y_own, u_own, t_own, y_all, u_all,
    go, load_sem, m_send, m_recv, y_send, y_recv, p_send, p_recv, g_send, g_recv,
):
    row = lax.axis_index("row")
    col = lax.axis_index("col")
    level = row // PER
    z = row % PER
    x = col // 2
    solver = col % 2 == 1

    load_d = pltpu.make_async_copy(inverse.at[row], d_in, load_sem.at[0])
    load_b = pltpu.make_async_copy(rhs.at[0, 0], b_in, load_sem.at[1])
    load_l = [pltpu.make_async_copy(factor.at[0, 0, k, 0], l_in.at[k], load_sem.at[2 + k]) for k in range(LEVELS - 1)]
    load_d.start()
    load_l[0].start()

    def peer(dx, h):
        return lax.rem(x + dx, SLICES) * 2 + h

    barrier = pltpu.get_barrier_semaphore()

    def signal(to_row, to_col):
        pl.semaphore_signal(barrier, inc=1, device_id=(to_row, to_col), device_id_type=MESH)

    @pl.when(solver & (level == 1))
    def _():
        for dz in FAR_FIRST:
            signal(lax.rem(z + dz, PER), peer(0, 1))

    @pl.when(solver & (level > 0))
    def _():
        for dz in FAR_FIRST:
            signal(lax.rem(z + dz, PER), peer(0, 0))

    @pl.when(solver)
    def _():
        for dx in (2, 1, 3):
            signal(row, peer(dx, 1))
        for dx in (2, 1, 3, 0):
            signal(row, peer(dx, 0))

    @pl.when(jnp.logical_not(solver))
    def _():
        for dx in (2, 1, 3, 0):
            signal(row, peer(dx, 1))

    load_b.start()
    for k in range(1, LEVELS - 1):
        load_l[k].start()

    def wait(ref, sem):
        pltpu.make_async_copy(ref, ref, sem).wait()

    def send(src, dst, ssem, rsem, to_row, to_col):
        pltpu.make_async_remote_copy(
            src_ref=src, dst_ref=dst, send_sem=ssem, recv_sem=rsem, device_id=(to_row, to_col), device_id_type=MESH
        ).start()

    def to_level(src_of, dst, ssem, rsem, target):
        for dz in FAR_FIRST:
            zt = lax.rem(z + dz, PER)
            send(src_of(zt), dst, ssem, rsem, target * PER + zt, col)

    def to_row(own, all_, which):
        all_[x] = own[...]
        for dx, h in ((2, 0), (2, 1), (1, 0), (3, 0), (1, 1), (3, 1), (0, 0)):
            send(own, all_.at[x], g_send.at[which], g_recv.at[which], row, peer(dx, h))

    load_d.wait()
    dh_, dl_ = halves(d_in[...])
    d_hl[:W, :] = dh_
    d_hl[W:, :] = dl_

    def form(k):
        load_l[k].wait()
        lh, ll = halves(l_in[k] * pattern[0, k].astype(F32))
        m_in[k, col] = quadrants(dot_nn(d_hl[...], jnp.concatenate([lh, ll], axis=1)), W, W)

    def turn():
        th, tl = halves(jnp.transpose(d_in[...]))
        dt_hl[:W, :] = th
        dt_hl[W:, :] = tl

    def finish(messages):
        wait(y_all.at[pl.ds(0, messages)], g_recv.at[0])
        y_out[0, 0] = jnp.transpose(y_all[...].reshape(W, W))
        wait(u_all.at[pl.ds(0, messages)], g_recv.at[1])
        ah, al = halves(u_all[...].reshape(W, W))
        x_out[0, 0] = quadrants(dot_nt(dt_hl[...], jnp.concatenate([ah, al], axis=0)), W, W)

    @pl.when(jnp.logical_not(solver))
    def _():
        for k in range(LEVELS - 1):

            @pl.when(level > k)
            def _(k=k):
                form(k)
                if k == 0:
                    pl.semaphore_wait(barrier, SLICES)
                own = m_in.at[k, col]
                for dx in (2, 1, 3, 0):
                    send(own, own, m_send, m_recv.at[k], row, peer(dx, 1))

            @pl.when(level <= k)
            def _(k=k):
                load_l[k].wait()

        @pl.when(level == 0)
        def _():
            pl.semaphore_wait(barrier, SLICES + 3 * PER)
            for to in (row, PER + row):
                pl.semaphore_signal(go, inc=1, device_id=(to, peer(0, 1)), device_id_type=MESH)

        load_b.wait()
        turn()
        finish(SLICES)
        for k in range(LEVELS - 1):

            @pl.when(level > k)
            def _(k=k):
                wait(m_in.at[k, pl.ds(0, SLICES)], m_send)

    def first_term():
        load_b.wait()
        b_t[...] = jnp.transpose(b_in[...])
        bh, bl = halves(b_t[pl.ds(pl.multiple_of(x * S, S), S), :])
        return quadrants(dot_nt(jnp.concatenate([bh, bl], axis=0), d_hl[...]), S, W)

    for lev in range(LEVELS):

        @pl.when(solver & (level == lev))
        def _(lev=lev):
            if lev == 0:
                start = first_term()
                y_own[...] = start
                pl.semaphore_wait(barrier, 7 + PER)
                for target in range(1, LEVELS):
                    if target == 2:
                        pl.semaphore_wait(go, 1)
                    to_level(lambda zt: y_own, y_in.at[0, z], y_send, y_recv.at[0], target)
            for k in range(lev, LEVELS - 1):
                load_l[k].wait()
            for k in range(lev):
                form(k)
                if k == 0:
                    pl.semaphore_wait(barrier, 7)
                own = m_in.at[k, col]
                for dx in (2, 1, 3):
                    send(own, own, m_send, m_recv.at[k], row, peer(dx, 1))
            if lev > 0:
                start = first_term()
            turn()
            for k in range(lev):
                wait(m_in.at[k, pl.ds(0, PER - 1)], m_recv.at[k])
                for c in range(PER):
                    mh, ml = halves(jnp.transpose(m_in[k, c]))
                    m_fwd[k, c * W:(c + 1) * W, :W] = mh
                    m_fwd[k, c * W:(c + 1) * W, W:] = ml
            acc = start
            for k in range(lev):
                wait(y_in.at[k], y_recv.at[k])
                parts = [halves(y_in[k, c]) for c in range(PER)]
                lhs = jnp.concatenate(
                    [jnp.concatenate([p[0] for p in parts], axis=1), jnp.concatenate([p[1] for p in parts], axis=1)], axis=0
                )
                acc = acc - quadrants(dot_nn(lhs, m_fwd[k]), S, W)
            if lev > 0:
                y_own[...] = acc
                if lev == 1:
                    pl.semaphore_wait(go, 1)
                for target in range(lev + 1, LEVELS):
                    to_level(lambda zt: y_own, y_in.at[lev, z], y_send, y_recv.at[lev], target)
            if lev < LEVELS - 1:
                to_row(y_own, y_all, 0)
            for k in range(lev):
                for c in range(PER):
                    mh, ml = halves(m_in[k, c])
                    m_bwd[k, :W, c * W:(c + 1) * W] = mh
                    m_bwd[k, W:, c * W:(c + 1) * W] = ml
            for up in range(LEVELS - 1, lev, -1):
                wait(p_in.at[up - 1], p_recv.at[up - 1])
                total = p_in[up - 1, 0]
                for c in range(1, PER):
                    total = total + p_in[up - 1, c]
                acc = acc - total
            u_own[...] = acc
            uh, ul = halves(acc)
            lhs = jnp.concatenate(
                [jnp.concatenate([uh, uh], axis=1), jnp.concatenate([ul, jnp.zeros_like(ul)], axis=1)], axis=0
            )
            for k in range(lev - 1, -1, -1):
                t = dot_nn(lhs, m_bwd[k])
                t = t[:S] + t[S:]
                for c in range(PER):
                    t_own[k, c] = t[:, c * W:(c + 1) * W]
                to_level(lambda zt: t_own.at[k, zt], p_in.at[lev - 1, z], p_send, p_recv.at[lev - 1], k)
            if lev == LEVELS - 1:
                to_row(y_own, y_all, 0)
            to_row(u_own, u_all, 1)
            finish(SLICES - 1)

            for k in range(lev):
                wait(m_in.at[k, pl.ds(0, SLICES - 1)], m_send)
                wait(t_own.at[k], p_send)
            for _ in range(lev + 1, LEVELS):
                wait(y_in.at[0], y_send)
            for which in range(2):
                wait(y_in.at[0, pl.ds(0, 7)], g_send.at[which])


def put(y, x, y_out, x_out, sem):
    a = pltpu.make_async_copy(y, y_out, sem.at[0])
    b = pltpu.make_async_copy(x, x_out, sem.at[1])
    a.start()
    b.start()
    a.wait()
    b.wait()


def shards(factor, pattern, inverse, rhs):
    out = jax.ShapeDtypeStruct((1, 1, W, W), F32)
    dma = pltpu.SemaphoreType.DMA
    y, x = pl.pallas_call(
        kernel,
        out_shape=(out, out),
        in_specs=[
            pl.BlockSpec(memory_space=pltpu.HBM),
            pl.BlockSpec(memory_space=pltpu.SMEM),
            pl.BlockSpec(memory_space=pltpu.HBM),
            pl.BlockSpec(memory_space=pltpu.HBM),
        ],
        out_specs=(pl.BlockSpec(memory_space=pltpu.VMEM), pl.BlockSpec(memory_space=pltpu.VMEM)),
        scratch_shapes=[
            pltpu.VMEM((W, W), F32),
            pltpu.VMEM((LEVELS - 1, W, W), F32),
            pltpu.VMEM((W, W), F32),
            pltpu.VMEM((W, W), F32),
            pltpu.VMEM((LEVELS - 1, PER, W, W), F32),
            pltpu.VMEM((LEVELS - 1, PER * W, 2 * W), BF16),
            pltpu.VMEM((LEVELS - 1, 2 * W, PER * W), BF16),
            pltpu.VMEM((2 * W, W), BF16),
            pltpu.VMEM((2 * W, W), BF16),
            pltpu.VMEM((LEVELS - 1, PER, S, W), F32),
            pltpu.VMEM((LEVELS - 1, PER, S, W), F32),
            pltpu.VMEM((S, W), F32),
            pltpu.VMEM((S, W), F32),
            pltpu.VMEM((LEVELS - 1, PER, S, W), F32),
            pltpu.VMEM((SLICES, S, W), F32),
            pltpu.VMEM((SLICES, S, W), F32),
            pltpu.SemaphoreType.REGULAR,
            dma((LEVELS + 1,)),
            dma,
            dma((LEVELS - 1,)),
            dma,
            dma((LEVELS - 1,)),
            dma,
            dma((LEVELS - 1,)),
            dma((2,)),
            dma((2,)),
        ],
        compiler_params=pltpu.CompilerParams(collective_id=0, has_side_effects=True, vmem_limit_bytes=60 * 2**20),
        name="solve",
    )(factor, pattern.reshape(1, LEVELS), inverse, rhs)
    return pl.pallas_call(
        put,
        out_shape=(out, out),
        in_specs=[pl.BlockSpec(memory_space=pltpu.VMEM)] * 2,
        out_specs=(pl.BlockSpec(memory_space=pltpu.HBM),) * 2,
        scratch_shapes=[dma((2,))],
        name="put",
    )(y, x)


def solution(mesh):
    return jax.shard_map(
        shards,
        mesh=mesh,
        in_specs=(
            P(None, "row", None, "col", None, None),
            P(None, "row", None, "col"),
            P(),
            P(None, "row", None, None),
        ),
        out_specs=(P(None, "row", None, None), P(None, "row", None, None)),
        check_vma=False,
    )
```

```python
import jax
import jax.numpy as jnp
from jax import lax
from jax.experimental import pallas as pl
from jax.experimental.pallas import tpu as pltpu
from jax.sharding import PartitionSpec as P

MESH = pl.DeviceIdType.MESH
F32 = jnp.float32
BF16 = jnp.bfloat16
LEVELS = 4
PER = 8
W = 128
SLICES = 4
S = W // SLICES
FAR_FIRST = (4, 3, 5, 2, 6, 1, 7, 0)


def halves(v):
    hi = v.astype(BF16)
    lo = (v - hi.astype(F32)).astype(BF16)
    return hi, lo


def quadrants(p, m, n):
    return p[:m, :n] + (p[m:, :n] + p[:m, n:])


def dot_nt(a, b):
    return lax.dot_general(a, b, (((1,), (1,)), ((), ())), preferred_element_type=F32)


def dot_nn(a, b):
    return lax.dot_general(a, b, (((1,), (0,)), ((), ())), preferred_element_type=F32)


def kernel(
    factor, pattern, inverse, rhs, y_out, x_out,
    d_in, l_in, b_in, b_t, m_in, m_fwd, m_bwd, d_hl, dt_hl, y_in, p_in, y_own, u_own, t_own, y_all, u_all,
    go, load_sem, m_send, m_recv, y_send, y_recv, p_send, p_recv, g_send, g_recv,
):
    row = lax.axis_index("row")
    col = lax.axis_index("col")
    level = row // PER
    z = row % PER
    x = col // 2
    solver = col % 2 == 1

    load_d = pltpu.make_async_copy(inverse.at[row], d_in, load_sem.at[0])
    load_b = pltpu.make_async_copy(rhs.at[0, 0], b_in, load_sem.at[1])
    load_l = [pltpu.make_async_copy(factor.at[0, 0, k, 0], l_in.at[k], load_sem.at[2 + k]) for k in range(LEVELS - 1)]
    load_d.start()
    load_l[0].start()

    def peer(dx, h):
        return lax.rem(x + dx, SLICES) * 2 + h

    barrier = pltpu.get_barrier_semaphore()

    def signal(to_row, to_col):
        pl.semaphore_signal(barrier, inc=1, device_id=(to_row, to_col), device_id_type=MESH)

    @pl.when(solver & (level == 1))
    def _():
        for dz in FAR_FIRST:
            signal(lax.rem(z + dz, PER), peer(0, 1))

    @pl.when(solver & (level > 0))
    def _():
        for dz in FAR_FIRST:
            signal(lax.rem(z + dz, PER), peer(0, 0))

    @pl.when(solver)
    def _():
        for dx in (2, 1, 3):
            signal(row, peer(dx, 1))
        for dx in (2, 1, 3, 0):
            signal(row, peer(dx, 0))

    @pl.when(jnp.logical_not(solver))
    def _():
        for dx in (2, 1, 3, 0):
            signal(row, peer(dx, 1))

    load_b.start()
    for k in range(1, LEVELS - 1):
        load_l[k].start()

    def wait(ref, sem):
        pltpu.make_async_copy(ref, ref, sem).wait()

    def send(src, dst, ssem, rsem, to_row, to_col):
        pltpu.make_async_remote_copy(
            src_ref=src, dst_ref=dst, send_sem=ssem, recv_sem=rsem, device_id=(to_row, to_col), device_id_type=MESH
        ).start()

    def to_level(src_of, dst, ssem, rsem, target, slots=range(PER)):
        for i in slots:
            zt = lax.rem(z + FAR_FIRST[i], PER)
            send(src_of(i), dst.at[i], ssem, rsem.at[min(i, 1)], target * PER + zt, col)

    def wait_near(ref, sem):
        wait(ref.at[pl.ds(1, PER - 1)], sem.at[1])

    def wait_far(ref, sem):
        wait(ref.at[0], sem.at[0])

    def to_row(own, all_, which):
        all_[x] = own[...]
        for dx, h in ((2, 0), (2, 1), (1, 0), (3, 0), (1, 1), (3, 1), (0, 0)):
            send(own, all_.at[x], g_send.at[which], g_recv.at[which], row, peer(dx, h))

    load_d.wait()
    dh_, dl_ = halves(d_in[...])
    d_hl[:W, :] = dh_
    d_hl[W:, :] = dl_

    def form(k):
        load_l[k].wait()
        lh, ll = halves(l_in[k] * pattern[0, k].astype(F32))
        m_in[k, col] = quadrants(dot_nn(d_hl[...], jnp.concatenate([lh, ll], axis=1)), W, W)

    def turn():
        th, tl = halves(jnp.transpose(d_in[...]))
        dt_hl[:W, :] = th
        dt_hl[W:, :] = tl

    def finish(messages):
        wait(y_all.at[pl.ds(0, messages)], g_recv.at[0])
        y_out[0, 0] = jnp.transpose(y_all[...].reshape(W, W))
        wait(u_all.at[pl.ds(0, messages)], g_recv.at[1])
        ah, al = halves(u_all[...].reshape(W, W))
        x_out[0, 0] = quadrants(dot_nt(dt_hl[...], jnp.concatenate([ah, al], axis=0)), W, W)

    @pl.when(jnp.logical_not(solver))
    def _():
        for k in range(LEVELS - 1):

            @pl.when(level > k)
            def _(k=k):
                form(k)
                if k == 0:
                    pl.semaphore_wait(barrier, SLICES)
                own = m_in.at[k, col]
                for dx in (2, 1, 3, 0):
                    send(own, own, m_send, m_recv.at[k], row, peer(dx, 1))

            @pl.when(level <= k)
            def _(k=k):
                load_l[k].wait()

        @pl.when(level == 0)
        def _():
            pl.semaphore_wait(barrier, SLICES + 3 * PER)
            for to in (row, PER + row):
                pl.semaphore_signal(go, inc=1, device_id=(to, peer(0, 1)), device_id_type=MESH)

        load_b.wait()
        turn()
        finish(SLICES)
        for k in range(LEVELS - 1):

            @pl.when(level > k)
            def _(k=k):
                wait(m_in.at[k, pl.ds(0, SLICES)], m_send)

    def first_term():
        load_b.wait()
        b_t[...] = jnp.transpose(b_in[...])
        bh, bl = halves(b_t[pl.ds(pl.multiple_of(x * S, S), S), :])
        return quadrants(dot_nt(jnp.concatenate([bh, bl], axis=0), d_hl[...]), S, W)

    for lev in range(LEVELS):

        @pl.when(solver & (level == lev))
        def _(lev=lev):
            if lev == 0:
                start = first_term()
                y_own[...] = start
                pl.semaphore_wait(barrier, 7 + PER)
                for target in range(1, LEVELS):
                    if target == 2:
                        pl.semaphore_wait(go, 1)
                    to_level(lambda i: y_own, y_in.at[0], y_send, y_recv.at[0], target)
            for k in range(lev, LEVELS - 1):
                load_l[k].wait()
            for k in range(lev):
                form(k)
                if k == 0:
                    pl.semaphore_wait(barrier, 7)
                own = m_in.at[k, col]
                for dx in (2, 1, 3):
                    send(own, own, m_send, m_recv.at[k], row, peer(dx, 1))
            if lev > 0:
                start = first_term()
            turn()
            for k in range(lev):
                wait(m_in.at[k, pl.ds(0, PER - 1)], m_recv.at[k])
                for i in range(PER):
                    mh, ml = halves(jnp.transpose(m_in[k, lax.rem(z + PER - FAR_FIRST[i], PER)]))
                    m_fwd[k, i * W:(i + 1) * W, :W] = mh
                    m_fwd[k, i * W:(i + 1) * W, W:] = ml
            acc = start
            for k in range(lev):
                wait_near(y_in.at[k], y_recv.at[k])
                parts = [halves(y_in[k, i]) for i in range(1, PER)]
                lhs = jnp.concatenate(
                    [jnp.concatenate([p[0] for p in parts], axis=1), jnp.concatenate([p[1] for p in parts], axis=1)], axis=0
                )
                acc = acc - quadrants(dot_nn(lhs, m_fwd[k, W:]), S, W)
                wait_far(y_in.at[k], y_recv.at[k])
                lhs = jnp.concatenate(halves(y_in[k, 0]), axis=0)
                acc = acc - quadrants(dot_nn(lhs, m_fwd[k, :W]), S, W)
            if lev > 0:
                y_own[...] = acc
                if lev == 1:
                    pl.semaphore_wait(go, 1)
                for target in range(lev + 1, LEVELS):
                    to_level(lambda i: y_own, y_in.at[lev], y_send, y_recv.at[lev], target)
            if lev < LEVELS - 1:
                to_row(y_own, y_all, 0)
            for k in range(lev):
                for i in range(PER):
                    mh, ml = halves(m_in[k, lax.rem(z + FAR_FIRST[i], PER)])
                    m_bwd[k, :W, i * W:(i + 1) * W] = mh
                    m_bwd[k, W:, i * W:(i + 1) * W] = ml
            for up in range(LEVELS - 1, lev, -1):
                wait_near(p_in.at[up - 1], p_recv.at[up - 1])
                total = p_in[up - 1, 1]
                for i in range(2, PER):
                    total = total + p_in[up - 1, i]
                acc = acc - total
                wait_far(p_in.at[up - 1], p_recv.at[up - 1])
                acc = acc - p_in[up - 1, 0]
            u_own[...] = acc
            uh, ul = halves(acc)
            lhs = jnp.concatenate(
                [jnp.concatenate([uh, uh], axis=1), jnp.concatenate([ul, jnp.zeros_like(ul)], axis=1)], axis=0
            )
            for k in range(lev - 1, -1, -1):
                t = dot_nn(lhs, m_bwd[k])
                t = t[:S] + t[S:]
                for c in range(PER):
                    t_own[k, c] = t[:, c * W:(c + 1) * W]
                to_level(lambda i: t_own.at[k, i], p_in.at[lev - 1], p_send, p_recv.at[lev - 1], k)
            if lev == LEVELS - 1:
                to_row(y_own, y_all, 0)
            to_row(u_own, u_all, 1)
            finish(SLICES - 1)

            for k in range(lev):
                wait(m_in.at[k, pl.ds(0, SLICES - 1)], m_send)
                wait(t_own.at[k], p_send)
            for _ in range(lev + 1, LEVELS):
                wait(y_in.at[0], y_send)
            for which in range(2):
                wait(y_in.at[0, pl.ds(0, 7)], g_send.at[which])


def put(y, x, y_out, x_out, sem):
    a = pltpu.make_async_copy(y, y_out, sem.at[0])
    b = pltpu.make_async_copy(x, x_out, sem.at[1])
    a.start()
    b.start()
    a.wait()
    b.wait()


def shards(factor, pattern, inverse, rhs):
    out = jax.ShapeDtypeStruct((1, 1, W, W), F32)
    dma = pltpu.SemaphoreType.DMA
    y, x = pl.pallas_call(
        kernel,
        out_shape=(out, out),
        in_specs=[
            pl.BlockSpec(memory_space=pltpu.HBM),
            pl.BlockSpec(memory_space=pltpu.SMEM),
            pl.BlockSpec(memory_space=pltpu.HBM),
            pl.BlockSpec(memory_space=pltpu.HBM),
        ],
        out_specs=(pl.BlockSpec(memory_space=pltpu.VMEM), pl.BlockSpec(memory_space=pltpu.VMEM)),
        scratch_shapes=[
            pltpu.VMEM((W, W), F32),
            pltpu.VMEM((LEVELS - 1, W, W), F32),
            pltpu.VMEM((W, W), F32),
            pltpu.VMEM((W, W), F32),
            pltpu.VMEM((LEVELS - 1, PER, W, W), F32),
            pltpu.VMEM((LEVELS - 1, PER * W, 2 * W), BF16),
            pltpu.VMEM((LEVELS - 1, 2 * W, PER * W), BF16),
            pltpu.VMEM((2 * W, W), BF16),
            pltpu.VMEM((2 * W, W), BF16),
            pltpu.VMEM((LEVELS - 1, PER, S, W), F32),
            pltpu.VMEM((LEVELS - 1, PER, S, W), F32),
            pltpu.VMEM((S, W), F32),
            pltpu.VMEM((S, W), F32),
            pltpu.VMEM((LEVELS - 1, PER, S, W), F32),
            pltpu.VMEM((SLICES, S, W), F32),
            pltpu.VMEM((SLICES, S, W), F32),
            pltpu.SemaphoreType.REGULAR,
            dma((LEVELS + 1,)),
            dma,
            dma((LEVELS - 1,)),
            dma,
            dma((LEVELS - 1, 2)),
            dma,
            dma((LEVELS - 1, 2)),
            dma((2,)),
            dma((2,)),
        ],
        compiler_params=pltpu.CompilerParams(collective_id=0, has_side_effects=True, vmem_limit_bytes=60 * 2**20),
        name="solve",
    )(factor, pattern.reshape(1, LEVELS), inverse, rhs)
    return pl.pallas_call(
        put,
        out_shape=(out, out),
        in_specs=[pl.BlockSpec(memory_space=pltpu.VMEM)] * 2,
        out_specs=(pl.BlockSpec(memory_space=pltpu.HBM),) * 2,
        scratch_shapes=[dma((2,))],
        name="put",
    )(y, x)


def solution(mesh):
    return jax.shard_map(
        shards,
        mesh=mesh,
        in_specs=(
            P(None, "row", None, "col", None, None),
            P(None, "row", None, "col"),
            P(),
            P(None, "row", None, None),
        ),
        out_specs=(P(None, "row", None, None), P(None, "row", None, None)),
        check_vma=False,
    )
```

```python
import jax
import jax.numpy as jnp
from jax import lax
from jax.experimental import pallas as pl
from jax.experimental.pallas import tpu as pltpu
from jax.sharding import PartitionSpec as P

MESH = pl.DeviceIdType.MESH
F32 = jnp.float32
BF16 = jnp.bfloat16
LEVELS = 4
PER = 8
W = 128
SLICES = 4
S = W // SLICES
FAR_FIRST = (4, 3, 5, 2, 6, 1, 7, 0)


def halves(v):
    hi = v.astype(BF16)
    lo = (v - hi.astype(F32)).astype(BF16)
    return hi, lo


def quadrants(p, m, n):
    return p[:m, :n] + (p[m:, :n] + p[:m, n:])


def dot_nt(a, b):
    return lax.dot_general(a, b, (((1,), (1,)), ((), ())), preferred_element_type=F32)


def dot_nn(a, b):
    return lax.dot_general(a, b, (((1,), (0,)), ((), ())), preferred_element_type=F32)


def kernel(
    factor, pattern, inverse, rhs, y_out, x_out,
    d_in, l_in, b_in, b_t, m_in, m_fwd, m_bwd, d_hl, dt_hl, y_in, p_in, y_own, u_own, t_own, y_all, u_all,
    go, load_sem, m_send, m_recv, y_send, y_recv, p_send, p_recv, g_send, g_recv,
):
    row = lax.axis_index("row")
    col = lax.axis_index("col")
    level = row // PER
    z = row % PER
    x = col // 2
    solver = col % 2 == 1

    load_d = pltpu.make_async_copy(inverse.at[row], d_in, load_sem.at[0])
    load_b = pltpu.make_async_copy(rhs.at[0, 0], b_in, load_sem.at[1])
    load_l = [pltpu.make_async_copy(factor.at[0, 0, k, 0], l_in.at[k], load_sem.at[2 + k]) for k in range(LEVELS - 1)]
    load_d.start()
    load_l[0].start()

    def peer(dx, h):
        return lax.rem(x + dx, SLICES) * 2 + h

    barrier = pltpu.get_barrier_semaphore()

    def signal(to_row, to_col):
        pl.semaphore_signal(barrier, inc=1, device_id=(to_row, to_col), device_id_type=MESH)

    @pl.when(solver & (level == 1))
    def _():
        for dz in FAR_FIRST:
            signal(lax.rem(z + dz, PER), peer(0, 1))

    @pl.when(solver & (level > 0))
    def _():
        for dz in FAR_FIRST:
            signal(lax.rem(z + dz, PER), peer(0, 0))

    @pl.when(solver)
    def _():
        for dx in (2, 1, 3):
            signal(row, peer(dx, 1))
        for dx in (2, 1, 3, 0):
            signal(row, peer(dx, 0))

    @pl.when(jnp.logical_not(solver))
    def _():
        for dx in (2, 1, 3, 0):
            signal(row, peer(dx, 1))

    load_b.start()
    for k in range(1, LEVELS - 1):
        load_l[k].start()

    def wait(ref, sem):
        pltpu.make_async_copy(ref, ref, sem).wait()

    def send(src, dst, ssem, rsem, to_row, to_col):
        pltpu.make_async_remote_copy(
            src_ref=src, dst_ref=dst, send_sem=ssem, recv_sem=rsem, device_id=(to_row, to_col), device_id_type=MESH
        ).start()

    def to_level(src_of, dst, ssem, rsem, target, slots=range(PER)):
        for i in slots:
            zt = lax.rem(z + FAR_FIRST[i], PER)
            send(src_of(i), dst.at[i], ssem, rsem.at[min(i, 1)], target * PER + zt, col)

    def wait_near(ref, sem):
        wait(ref.at[pl.ds(1, PER - 1)], sem.at[1])

    def wait_far(ref, sem):
        wait(ref.at[0], sem.at[0])

    def to_row(own, all_, which):
        all_[x] = own[...]
        for dx, h in ((2, 0), (2, 1), (1, 0), (3, 0), (1, 1), (3, 1), (0, 0)):
            send(own, all_.at[x], g_send.at[which], g_recv.at[which], row, peer(dx, h))

    load_d.wait()
    dh_, dl_ = halves(d_in[...])
    d_hl[:W, :] = dh_
    d_hl[W:, :] = dl_

    def form(k):
        load_l[k].wait()
        lh, ll = halves(l_in[k] * pattern[0, k].astype(F32))
        m_in[k, col] = quadrants(dot_nn(d_hl[...], jnp.concatenate([lh, ll], axis=1)), W, W)

    def turn():
        th, tl = halves(jnp.transpose(d_in[...]))
        dt_hl[:W, :] = th
        dt_hl[W:, :] = tl

    def finish(messages):
        wait(y_all.at[pl.ds(0, messages)], g_recv.at[0])
        y_out[0, 0] = jnp.transpose(y_all[...].reshape(W, W))
        wait(u_all.at[pl.ds(0, messages)], g_recv.at[1])
        ah, al = halves(u_all[...].reshape(W, W))
        x_out[0, 0] = quadrants(dot_nt(dt_hl[...], jnp.concatenate([ah, al], axis=0)), W, W)

    @pl.when(jnp.logical_not(solver))
    def _():
        for k in range(LEVELS - 1):

            @pl.when(level > k)
            def _(k=k):
                form(k)
                if k == 0:
                    pl.semaphore_wait(barrier, SLICES)
                own = m_in.at[k, col]
                for dx in (2, 1, 3, 0):
                    send(own, own, m_send, m_recv.at[k], row, peer(dx, 1))

            @pl.when(level <= k)
            def _(k=k):
                load_l[k].wait()

        @pl.when(level == 0)
        def _():
            pl.semaphore_wait(barrier, SLICES + 3 * PER)
            for to in (row, PER + row):
                pl.semaphore_signal(go, inc=1, device_id=(to, peer(0, 1)), device_id_type=MESH)

        load_b.wait()
        turn()
        finish(SLICES)
        for k in range(LEVELS - 1):

            @pl.when(level > k)
            def _(k=k):
                wait(m_in.at[k, pl.ds(0, SLICES)], m_send)

    def first_term():
        load_b.wait()
        b_t[...] = jnp.transpose(b_in[...])
        bh, bl = halves(b_t[pl.ds(pl.multiple_of(x * S, S), S), :])
        return quadrants(dot_nt(jnp.concatenate([bh, bl], axis=0), d_hl[...]), S, W)

    for lev in range(LEVELS):

        @pl.when(solver & (level == lev))
        def _(lev=lev):
            if lev == 0:
                start = first_term()
                y_own[...] = start
                pl.semaphore_wait(barrier, 7 + PER)
                for target in range(1, LEVELS):
                    if target == 2:
                        pl.semaphore_wait(go, 1)
                    to_level(lambda i: y_own, y_in.at[0], y_send, y_recv.at[0], target)
            for k in range(lev, LEVELS - 1):
                load_l[k].wait()
            for k in range(lev):
                form(k)
                if k == 0:
                    pl.semaphore_wait(barrier, 7)
                own = m_in.at[k, col]
                for dx in (2, 1, 3):
                    send(own, own, m_send, m_recv.at[k], row, peer(dx, 1))
            if lev > 0:
                start = first_term()
            turn()
            for k in range(lev):
                wait(m_in.at[k, pl.ds(0, PER - 1)], m_recv.at[k])
                for i in range(PER):
                    mh, ml = halves(jnp.transpose(m_in[k, lax.rem(z + PER - FAR_FIRST[i], PER)]))
                    m_fwd[k, i * W:(i + 1) * W, :W] = mh
                    m_fwd[k, i * W:(i + 1) * W, W:] = ml
            acc = start
            for k in range(lev):
                wait_near(y_in.at[k], y_recv.at[k])
                parts = [halves(y_in[k, i]) for i in range(1, PER)]
                lhs = jnp.concatenate(
                    [jnp.concatenate([p[0] for p in parts], axis=1), jnp.concatenate([p[1] for p in parts], axis=1)], axis=0
                )
                acc = acc - quadrants(dot_nn(lhs, m_fwd[k, W:]), S, W)
                wait_far(y_in.at[k], y_recv.at[k])
                lhs = jnp.concatenate(halves(y_in[k, 0]), axis=0)
                acc = acc - quadrants(dot_nn(lhs, m_fwd[k, :W]), S, W)
            if lev > 0:
                y_own[...] = acc
                if lev == 1:
                    pl.semaphore_wait(go, 1)
                for target in range(lev + 1, LEVELS):
                    to_level(lambda i: y_own, y_in.at[lev], y_send, y_recv.at[lev], target)
            if lev < LEVELS - 1:
                to_row(y_own, y_all, 0)
            for k in range(lev):
                for i in range(PER):
                    mh, ml = halves(m_in[k, lax.rem(z + FAR_FIRST[i], PER)])
                    m_bwd[k, :W, i * W:(i + 1) * W] = mh
                    m_bwd[k, W:, i * W:(i + 1) * W] = ml
            for up in range(LEVELS - 1, lev, -1):
                wait_near(p_in.at[up - 1], p_recv.at[up - 1])
                total = p_in[up - 1, 1]
                for i in range(2, PER):
                    total = total + p_in[up - 1, i]
                acc = acc - total
                wait_far(p_in.at[up - 1], p_recv.at[up - 1])
                acc = acc - p_in[up - 1, 0]
            u_own[...] = acc
            uh, ul = halves(acc)
            lhs = jnp.concatenate(
                [jnp.concatenate([uh, uh], axis=1), jnp.concatenate([ul, jnp.zeros_like(ul)], axis=1)], axis=0
            )
            for k in range(lev - 1, -1, -1):
                t = dot_nn(lhs, m_bwd[k])
                t = t[:S] + t[S:]
                for c in range(PER):
                    t_own[k, c] = t[:, c * W:(c + 1) * W]
                to_level(lambda i: t_own.at[k, i], p_in.at[lev - 1], p_send, p_recv.at[lev - 1], k)
            if lev == LEVELS - 1:
                to_row(y_own, y_all, 0)
            to_row(u_own, u_all, 1)
            finish(SLICES - 1)

            for k in range(lev):
                wait(m_in.at[k, pl.ds(0, SLICES - 1)], m_send)
                wait(t_own.at[k], p_send)
            for _ in range(lev + 1, LEVELS):
                wait(y_in.at[0], y_send)
            for which in range(2):
                wait(y_in.at[0, pl.ds(0, 7)], g_send.at[which])


def put(y, x, y_out, x_out, sem):
    a = pltpu.make_async_copy(y, y_out, sem.at[0])
    b = pltpu.make_async_copy(x, x_out, sem.at[1])
    a.start()
    b.start()
    a.wait()
    b.wait()


def shards(factor, pattern, inverse, rhs):
    out = jax.ShapeDtypeStruct((1, 1, W, W), F32)
    dma = pltpu.SemaphoreType.DMA
    y, x = pl.pallas_call(
        kernel,
        out_shape=(pltpu.VMEM((1, 1, W, W), F32),) * 2,
        in_specs=[
            pl.BlockSpec(memory_space=pltpu.HBM),
            pl.BlockSpec(memory_space=pltpu.SMEM),
            pl.BlockSpec(memory_space=pltpu.HBM),
            pl.BlockSpec(memory_space=pltpu.HBM),
        ],
        out_specs=(pl.BlockSpec(memory_space=pltpu.VMEM), pl.BlockSpec(memory_space=pltpu.VMEM)),
        scratch_shapes=[
            pltpu.VMEM((W, W), F32),
            pltpu.VMEM((LEVELS - 1, W, W), F32),
            pltpu.VMEM((W, W), F32),
            pltpu.VMEM((W, W), F32),
            pltpu.VMEM((LEVELS - 1, PER, W, W), F32),
            pltpu.VMEM((LEVELS - 1, PER * W, 2 * W), BF16),
            pltpu.VMEM((LEVELS - 1, 2 * W, PER * W), BF16),
            pltpu.VMEM((2 * W, W), BF16),
            pltpu.VMEM((2 * W, W), BF16),
            pltpu.VMEM((LEVELS - 1, PER, S, W), F32),
            pltpu.VMEM((LEVELS - 1, PER, S, W), F32),
            pltpu.VMEM((S, W), F32),
            pltpu.VMEM((S, W), F32),
            pltpu.VMEM((LEVELS - 1, PER, S, W), F32),
            pltpu.VMEM((SLICES, S, W), F32),
            pltpu.VMEM((SLICES, S, W), F32),
            pltpu.SemaphoreType.REGULAR,
            dma((LEVELS + 1,)),
            dma,
            dma((LEVELS - 1,)),
            dma,
            dma((LEVELS - 1, 2)),
            dma,
            dma((LEVELS - 1, 2)),
            dma((2,)),
            dma((2,)),
        ],
        compiler_params=pltpu.CompilerParams(collective_id=0, has_side_effects=True, vmem_limit_bytes=60 * 2**20),
        name="solve",
    )(factor, pattern.reshape(1, LEVELS), inverse, rhs)
    return pl.pallas_call(
        put,
        out_shape=(out, out),
        in_specs=[pl.BlockSpec(memory_space=pltpu.VMEM)] * 2,
        out_specs=(pl.BlockSpec(memory_space=pltpu.HBM),) * 2,
        scratch_shapes=[dma((2,))],
        name="put",
    )(pltpu.with_memory_space_constraint(y, pltpu.VMEM), pltpu.with_memory_space_constraint(x, pltpu.VMEM))


def solution(mesh):
    return jax.shard_map(
        shards,
        mesh=mesh,
        in_specs=(
            P(None, "row", None, "col", None, None),
            P(None, "row", None, "col"),
            P(),
            P(None, "row", None, None),
        ),
        out_specs=(P(None, "row", None, None), P(None, "row", None, None)),
        check_vma=False,
    )
```

```python
import jax
import jax.numpy as jnp
from jax import lax
from jax.experimental import pallas as pl
from jax.experimental.pallas import tpu as pltpu
from jax.sharding import PartitionSpec as P

MESH = pl.DeviceIdType.MESH
F32 = jnp.float32
BF16 = jnp.bfloat16
LEVELS = 4
PER = 8
W = 128
SLICES = 4
S = W // SLICES
FAR_FIRST = (4, 3, 5, 2, 6, 1, 7, 0)


def halves(v):
    hi = v.astype(BF16)
    lo = (v - hi.astype(F32)).astype(BF16)
    return hi, lo


def quadrants(p, m, n):
    return p[:m, :n] + (p[m:, :n] + p[:m, n:])


def dot_nt(a, b):
    return lax.dot_general(a, b, (((1,), (1,)), ((), ())), preferred_element_type=F32)


def dot_nn(a, b):
    return lax.dot_general(a, b, (((1,), (0,)), ((), ())), preferred_element_type=F32)


def kernel(
    factor, pattern, inverse, rhs, y_out, x_out,
    d_in, l_in, b_in, b_t, m_in, m_fwd, m_bwd, d_hl, dt_hl, y_in, p_in, y_own, u_own, t_own, y_all, u_all,
    kept, go, load_sem, m_send, m_recv, y_send, y_recv, p_send, p_recv, g_send, g_recv,
):
    row = lax.axis_index("row")
    col = lax.axis_index("col")
    level = row // PER
    z = row % PER
    x = col // 2
    solver = col % 2 == 1

    load_d = pltpu.make_async_copy(inverse.at[row], d_in, load_sem.at[0])
    load_b = pltpu.make_async_copy(rhs.at[0, 0], b_in, load_sem.at[1])
    load_l = [pltpu.make_async_copy(factor.at[0, 0, k, 0], l_in.at[k], load_sem.at[2 + k]) for k in range(LEVELS - 1)]
    load_p = pltpu.make_async_copy(pattern, kept, load_sem.at[LEVELS + 1])
    load_d.start()
    load_l[0].start()
    load_p.start()

    def peer(dx, h):
        return lax.rem(x + dx, SLICES) * 2 + h

    barrier = pltpu.get_barrier_semaphore()

    def signal(to_row, to_col):
        pl.semaphore_signal(barrier, inc=1, device_id=(to_row, to_col), device_id_type=MESH)

    @pl.when(solver & (level == 1))
    def _():
        for dz in FAR_FIRST:
            signal(lax.rem(z + dz, PER), peer(0, 1))

    @pl.when(solver & (level > 0))
    def _():
        for dz in FAR_FIRST:
            signal(lax.rem(z + dz, PER), peer(0, 0))

    @pl.when(solver)
    def _():
        for dx in (2, 1, 3):
            signal(row, peer(dx, 1))
        for dx in (2, 1, 3, 0):
            signal(row, peer(dx, 0))

    @pl.when(jnp.logical_not(solver))
    def _():
        for dx in (2, 1, 3, 0):
            signal(row, peer(dx, 1))

    load_b.start()
    for k in range(1, LEVELS - 1):
        load_l[k].start()

    def wait(ref, sem):
        pltpu.make_async_copy(ref, ref, sem).wait()

    def send(src, dst, ssem, rsem, to_row, to_col):
        pltpu.make_async_remote_copy(
            src_ref=src, dst_ref=dst, send_sem=ssem, recv_sem=rsem, device_id=(to_row, to_col), device_id_type=MESH
        ).start()

    def to_level(src_of, dst, ssem, rsem, target, slots=range(PER)):
        for i in slots:
            zt = lax.rem(z + FAR_FIRST[i], PER)
            send(src_of(i), dst.at[i], ssem, rsem.at[min(i, 1)], target * PER + zt, col)

    def wait_near(ref, sem):
        wait(ref.at[pl.ds(1, PER - 1)], sem.at[1])

    def wait_far(ref, sem):
        wait(ref.at[0], sem.at[0])

    def to_row(own, all_, which):
        all_[x] = own[...]
        for dx, h in ((2, 0), (2, 1), (1, 0), (3, 0), (1, 1), (3, 1), (0, 0)):
            send(own, all_.at[x], g_send.at[which], g_recv.at[which], row, peer(dx, h))

    load_p.wait()
    load_d.wait()
    dh_, dl_ = halves(d_in[...])
    d_hl[:W, :] = dh_
    d_hl[W:, :] = dl_

    def form(k):
        load_l[k].wait()
        lh, ll = halves(l_in[k] * kept[0, k].astype(F32))
        m_in[k, col] = quadrants(dot_nn(d_hl[...], jnp.concatenate([lh, ll], axis=1)), W, W)

    def turn():
        th, tl = halves(jnp.transpose(d_in[...]))
        dt_hl[:W, :] = th
        dt_hl[W:, :] = tl

    def finish(messages):
        wait(y_all.at[pl.ds(0, messages)], g_recv.at[0])
        y_out[0, 0] = jnp.transpose(y_all[...].reshape(W, W))
        wait(u_all.at[pl.ds(0, messages)], g_recv.at[1])
        ah, al = halves(u_all[...].reshape(W, W))
        x_out[0, 0] = quadrants(dot_nt(dt_hl[...], jnp.concatenate([ah, al], axis=0)), W, W)

    @pl.when(jnp.logical_not(solver))
    def _():
        for k in range(LEVELS - 1):

            @pl.when(level > k)
            def _(k=k):
                form(k)
                if k == 0:
                    pl.semaphore_wait(barrier, SLICES)
                own = m_in.at[k, col]
                for dx in (2, 1, 3, 0):
                    send(own, own, m_send, m_recv.at[k], row, peer(dx, 1))

            @pl.when(level <= k)
            def _(k=k):
                load_l[k].wait()

        @pl.when(level == 0)
        def _():
            pl.semaphore_wait(barrier, SLICES + 3 * PER)
            for to in (row, PER + row):
                pl.semaphore_signal(go, inc=1, device_id=(to, peer(0, 1)), device_id_type=MESH)

        load_b.wait()
        turn()
        finish(SLICES)
        for k in range(LEVELS - 1):

            @pl.when(level > k)
            def _(k=k):
                wait(m_in.at[k, pl.ds(0, SLICES)], m_send)

    def first_term():
        load_b.wait()
        b_t[...] = jnp.transpose(b_in[...])
        bh, bl = halves(b_t[pl.ds(pl.multiple_of(x * S, S), S), :])
        return quadrants(dot_nt(jnp.concatenate([bh, bl], axis=0), d_hl[...]), S, W)

    for lev in range(LEVELS):

        @pl.when(solver & (level == lev))
        def _(lev=lev):
            if lev == 0:
                start = first_term()
                y_own[...] = start
                pl.semaphore_wait(barrier, 7 + PER)
                for target in range(1, LEVELS):
                    if target == 2:
                        pl.semaphore_wait(go, 1)
                    to_level(lambda i: y_own, y_in.at[0], y_send, y_recv.at[0], target)
            for k in range(lev, LEVELS - 1):
                load_l[k].wait()
            for k in range(lev):
                form(k)
                if k == 0:
                    pl.semaphore_wait(barrier, 7)
                own = m_in.at[k, col]
                for dx in (2, 1, 3):
                    send(own, own, m_send, m_recv.at[k], row, peer(dx, 1))
            if lev > 0:
                start = first_term()
            turn()
            for k in range(lev):
                wait(m_in.at[k, pl.ds(0, PER - 1)], m_recv.at[k])
                for i in range(PER):
                    mh, ml = halves(jnp.transpose(m_in[k, lax.rem(z + PER - FAR_FIRST[i], PER)]))
                    m_fwd[k, i * W:(i + 1) * W, :W] = mh
                    m_fwd[k, i * W:(i + 1) * W, W:] = ml
            acc = start
            for k in range(lev):
                wait_near(y_in.at[k], y_recv.at[k])
                parts = [halves(y_in[k, i]) for i in range(1, PER)]
                lhs = jnp.concatenate(
                    [jnp.concatenate([p[0] for p in parts], axis=1), jnp.concatenate([p[1] for p in parts], axis=1)], axis=0
                )
                acc = acc - quadrants(dot_nn(lhs, m_fwd[k, W:]), S, W)
                wait_far(y_in.at[k], y_recv.at[k])
                lhs = jnp.concatenate(halves(y_in[k, 0]), axis=0)
                acc = acc - quadrants(dot_nn(lhs, m_fwd[k, :W]), S, W)
            if lev > 0:
                y_own[...] = acc
                if lev == 1:
                    pl.semaphore_wait(go, 1)
                for target in range(lev + 1, LEVELS):
                    to_level(lambda i: y_own, y_in.at[lev], y_send, y_recv.at[lev], target)
            if lev < LEVELS - 1:
                to_row(y_own, y_all, 0)
            for k in range(lev):
                for i in range(PER):
                    mh, ml = halves(m_in[k, lax.rem(z + FAR_FIRST[i], PER)])
                    m_bwd[k, :W, i * W:(i + 1) * W] = mh
                    m_bwd[k, W:, i * W:(i + 1) * W] = ml
            for up in range(LEVELS - 1, lev, -1):
                wait_near(p_in.at[up - 1], p_recv.at[up - 1])
                total = p_in[up - 1, 1]
                for i in range(2, PER):
                    total = total + p_in[up - 1, i]
                acc = acc - total
                wait_far(p_in.at[up - 1], p_recv.at[up - 1])
                acc = acc - p_in[up - 1, 0]
            u_own[...] = acc
            uh, ul = halves(acc)
            lhs = jnp.concatenate(
                [jnp.concatenate([uh, uh], axis=1), jnp.concatenate([ul, jnp.zeros_like(ul)], axis=1)], axis=0
            )
            for k in range(lev - 1, -1, -1):
                t = dot_nn(lhs, m_bwd[k])
                t = t[:S] + t[S:]
                for c in range(PER):
                    t_own[k, c] = t[:, c * W:(c + 1) * W]
                to_level(lambda i: t_own.at[k, i], p_in.at[lev - 1], p_send, p_recv.at[lev - 1], k)
            if lev == LEVELS - 1:
                to_row(y_own, y_all, 0)
            to_row(u_own, u_all, 1)
            finish(SLICES - 1)

            for k in range(lev):
                wait(m_in.at[k, pl.ds(0, SLICES - 1)], m_send)
                wait(t_own.at[k], p_send)
            for _ in range(lev + 1, LEVELS):
                wait(y_in.at[0], y_send)
            for which in range(2):
                wait(y_in.at[0, pl.ds(0, 7)], g_send.at[which])


def put(y, x, y_out, x_out, sem):
    a = pltpu.make_async_copy(y, y_out, sem.at[0])
    b = pltpu.make_async_copy(x, x_out, sem.at[1])
    a.start()
    b.start()
    a.wait()
    b.wait()


def shards(factor, pattern, inverse, rhs):
    out = jax.ShapeDtypeStruct((1, 1, W, W), F32)
    dma = pltpu.SemaphoreType.DMA
    y, x = pl.pallas_call(
        kernel,
        out_shape=(pltpu.VMEM((1, 1, W, W), F32),) * 2,
        in_specs=[
            pl.BlockSpec(memory_space=pltpu.HBM),
            pl.BlockSpec(memory_space=pltpu.HBM),
            pl.BlockSpec(memory_space=pltpu.HBM),
            pl.BlockSpec(memory_space=pltpu.HBM),
        ],
        out_specs=(pl.BlockSpec(memory_space=pltpu.VMEM), pl.BlockSpec(memory_space=pltpu.VMEM)),
        scratch_shapes=[
            pltpu.VMEM((W, W), F32),
            pltpu.VMEM((LEVELS - 1, W, W), F32),
            pltpu.VMEM((W, W), F32),
            pltpu.VMEM((W, W), F32),
            pltpu.VMEM((LEVELS - 1, PER, W, W), F32),
            pltpu.VMEM((LEVELS - 1, PER * W, 2 * W), BF16),
            pltpu.VMEM((LEVELS - 1, 2 * W, PER * W), BF16),
            pltpu.VMEM((2 * W, W), BF16),
            pltpu.VMEM((2 * W, W), BF16),
            pltpu.VMEM((LEVELS - 1, PER, S, W), F32),
            pltpu.VMEM((LEVELS - 1, PER, S, W), F32),
            pltpu.VMEM((S, W), F32),
            pltpu.VMEM((S, W), F32),
            pltpu.VMEM((LEVELS - 1, PER, S, W), F32),
            pltpu.VMEM((SLICES, S, W), F32),
            pltpu.VMEM((SLICES, S, W), F32),
            pltpu.SMEM((1, LEVELS), jnp.int32),
            pltpu.SemaphoreType.REGULAR,
            dma((LEVELS + 2,)),
            dma,
            dma((LEVELS - 1,)),
            dma,
            dma((LEVELS - 1, 2)),
            dma,
            dma((LEVELS - 1, 2)),
            dma((2,)),
            dma((2,)),
        ],
        compiler_params=pltpu.CompilerParams(collective_id=0, has_side_effects=True, vmem_limit_bytes=60 * 2**20),
        name="solve",
    )(factor, pattern.reshape(1, LEVELS), inverse, rhs)
    return pl.pallas_call(
        put,
        out_shape=(out, out),
        in_specs=[pl.BlockSpec(memory_space=pltpu.VMEM)] * 2,
        out_specs=(pl.BlockSpec(memory_space=pltpu.HBM),) * 2,
        scratch_shapes=[dma((2,))],
        name="put",
    )(pltpu.with_memory_space_constraint(y, pltpu.VMEM), pltpu.with_memory_space_constraint(x, pltpu.VMEM))


def solution(mesh):
    return jax.shard_map(
        shards,
        mesh=mesh,
        in_specs=(
            P(None, "row", None, "col", None, None),
            P(None, "row", None, "col"),
            P(),
            P(None, "row", None, None),
        ),
        out_specs=(P(None, "row", None, None), P(None, "row", None, None)),
        check_vma=False,
    )
```
